512 devices in a mesh: ctx: 32 (over x_hi, z, core), tp: 16 (over y, x_lo).
Axes of the slice: x: 4 (x_hi: 2, x_lo: 2; x = x_hi * 2 + x_lo), y: 8, z: 8, core: 2. Of those that a mesh axis runs over, the one named last changes fastest.
Arguments:
- hidden: bfloat16 [12288, 8192], P('ctx', 'tp'), may hold values from -18 to 18
- counts: int32 [32], P('ctx'), may hold values from 1 to 384, 4096 in all
- positions: int32 [12288], P('ctx'), may hold values from 0 to 61439, as said below
- w_query: bfloat16 [8192, 4096], P('ctx', 'tp'), may hold values from -0.0625 to 0.0625
- key_value_weight: bfloat16 [8192, 1024], P('tp'), may hold values from -0.0625 to 0.0625
Outputs:
- attended: bfloat16 [4096, 4096], P('ctx', 'tp')
The draws below stay inside these ranges and needn't reach their ends.
Inputs may be any that keep to these rules, and one draw needn't show every extreme that they name: The counts sum to 4096; the largest is exactly 384. `positions`: strictly increasing along the array, consecutive entries 1 to 9 apart, the first 0.
All inputs are finite; a program needn't handle non-finite values. No bound on the sum of `counts` on one device may be relied on, other than what follows from the above.
Results may differ from the reference program's by a relative error of at most 0.035.
Values may be sent and summed in bfloat16 or wider, within the bound.
A program may use at most 64 MiB of HBM per device.

```python
import math
import jax
import jax.numpy as jnp
import numpy as np
from jax import lax

MODEL_WIDTH = 8192
HEAD_SIZE = 128
QUERY_HEADS = 32
KEY_VALUE_HEADS = 4
STRIDE = 5
ROWS_DEV = 128
CAP = 384
KEPT_ROW_TOTAL = 4096
N_CTX = 32


def draw_hidden(key, part):
    key = jax.random.fold_in(key, 11)
    row_count = N_CTX * CAP
    entries = jnp.clip(jax.random.normal(key, (row_count, MODEL_WIDTH), jnp.float32), -6.0, 6.0)
    return entries.astype(jnp.bfloat16)


def draw_positions(key, part):
    key = jax.random.fold_in(key, 5)
    slot_total = N_CTX * CAP
    jitter = jax.random.randint(key, (slot_total,), 0, STRIDE, dtype=jnp.int32)
    jitter = jitter.at[0].set(0).at[slot_total - 1].set(STRIDE - 1)
    return (jnp.arange(slot_total, dtype=jnp.int32) * STRIDE + jitter).astype(jnp.int32)


def level_of(key, shape, pieces, least, high):
    factor_of, own = 1.0, jax.random.fold_in(key, 6)
    for position, parts in pieces:
        draws = jnp.exp(jax.random.uniform(jax.random.fold_in(own, position), (parts,), jnp.float32, least / len(pieces), high / len(pieces)))
        factor_of = factor_of * jnp.repeat(draws, shape[position] // parts).reshape([-1 if axis == position else 1 for axis in range(len(shape))])
    return factor_of


def profile(number_of, total, most, slope):
    portions = [(1 << 20) // math.isqrt(standing ** slope) + 1 for standing in range(2, number_of + 1)]
    spare, given = total - most - (number_of - 1), [1] * (number_of - 1)
    while spare > 0:
        candidates = [i for i in range(number_of - 1) if given[i] < most]
        whole, budget = sum([portions[i] for i in candidates]), spare
        for i in candidates:
            more = min(most - given[i], max(1, budget * portions[i] // whole), spare)
            given[i] = given[i] + more
            spare = spare - more
    return np.array([most] + given)


def uneven_parts(key, amount, total, reach, lean):
    if amount == 2:
        one = jax.random.randint(key, (), max(1, total - reach), min(reach, total - 1) + 1)
        return jnp.stack([one, total - one])
    tallies = jnp.asarray(profile(amount, total, reach, lean), jnp.int32)
    couples = (amount - 1) // 2
    source_of, receiver = tallies[1:1 + 2 * couples:2], tallies[2:2 + 2 * couples:2]
    room = jnp.minimum(source_of - 1, reach - receiver)
    passed = jax.random.randint(jax.random.fold_in(key, 1), (couples,), 0, 1 << 20) % (room + 1)
    tallies = tallies.at[1:1 + 2 * couples:2].set(source_of - passed).at[2:2 + 2 * couples:2].set(receiver + passed)
    return tallies[jax.random.permutation(jax.random.fold_in(key, 2), amount)]


def normal_values(stream_key, dims, scale, limit, shards=(), kind=jnp.bfloat16):
    level = level_of(stream_key, dims, shards, -0.22, 0.18) if shards else 1.0
    array = jax.random.normal(stream_key, dims, jnp.float32) * scale * level
    return jnp.minimum(jnp.maximum(array, -limit), limit).astype(kind)


def setup_inputs(seed: int = 0) -> dict:
    arg_keys = jax.random.split(jax.random.key(seed), 6)
    return {
        "hidden": draw_hidden(jax.random.fold_in(arg_keys[5], 71), 0),
        "counts": uneven_parts(arg_keys[1], N_CTX, KEPT_ROW_TOTAL, CAP, 2).astype(jnp.int32),
        "positions": draw_positions(jax.random.fold_in(arg_keys[5], 71), 0),
        "w_query": normal_values(arg_keys[3], (MODEL_WIDTH, QUERY_HEADS * HEAD_SIZE), MODEL_WIDTH ** -0.5, 0.0625, ((0, 32), (1, 16))),
        "key_value_weight": normal_values(arg_keys[4], (MODEL_WIDTH, KEY_VALUE_HEADS * 2 * HEAD_SIZE), MODEL_WIDTH ** -0.5, 0.0625, ((0, 16),)),
    }


rope_base = 500000.0
masked_score = -1e+30
query_block = 512

def rope_angles(position_list, head_dim):
    half_dim = head_dim // 2
    exponent = jnp.arange(half_dim, dtype=jnp.float32) * (2.0 / head_dim)
    inverse = jnp.power(jnp.float32(rope_base), -exponent)
    return position_list.astype(jnp.float32)[:, None] * inverse[None, :]

def rotate(values, angles):
    half_dim = values.shape[-1] // 2
    cosine = jnp.cos(angles)
    sine_part = jnp.sin(angles)
    leading = values[..., :half_dim]
    trailing = values[..., half_dim:]
    return jnp.concatenate([leading * cosine - trailing * sine_part, trailing * cosine + leading * sine_part], axis=-1)

def kept_index(counts):
    offsets = (jnp.cumsum(counts) - counts).astype(jnp.int32)
    order = jnp.arange(KEPT_ROW_TOTAL, dtype=jnp.int32)
    ranks = (order % ROWS_DEV * N_CTX + order // ROWS_DEV).astype(jnp.int32)
    source = (lax.optimization_barrier(jnp.sum((offsets[None, :] <= ranks[:, None]).astype(jnp.int32), axis=1)) - 1).astype(jnp.int32)
    return (source * CAP + ranks - offsets[source]).astype(jnp.int32)

def reference(hidden, counts, positions, w_query, key_value_weight):
    flat_index = kept_index(counts)
    retained_rows = hidden[flat_index]
    kept_positions = positions[flat_index]
    angles = rope_angles(kept_positions, HEAD_SIZE)
    queries = jnp.dot(retained_rows, w_query, preferred_element_type=jnp.float32).reshape(KEPT_ROW_TOTAL, QUERY_HEADS, HEAD_SIZE)
    queries = rotate(queries, angles[:, None, :]).astype(jnp.bfloat16)
    key_value_rows = jnp.dot(retained_rows, key_value_weight, preferred_element_type=jnp.float32).reshape(KEPT_ROW_TOTAL, KEY_VALUE_HEADS, 2, HEAD_SIZE)
    keys = rotate(key_value_rows[:, :, 0], angles[:, None, :]).astype(jnp.bfloat16)
    values = key_value_rows[:, :, 1].astype(jnp.bfloat16)
    score_scale = 1.0 / math.sqrt(HEAD_SIZE)
    group_width = QUERY_HEADS // KEY_VALUE_HEADS
    block_rows = min(query_block, KEPT_ROW_TOTAL)
    block_count = KEPT_ROW_TOTAL // block_rows

    def one_head(head):
        key_head = keys[:, head // group_width]
        value_head = values[:, head // group_width]
        query_head = queries[:, head].reshape(block_count, block_rows, HEAD_SIZE)
        query_pos = kept_positions.reshape(block_count, block_rows)

        def one_block(pair):
            query_part, pos_part = pair
            causal = kept_positions[None, :] <= pos_part[:, None]
            scores = lax.dot_general(query_part, key_head, (((1,), (1,)), ((), ())), preferred_element_type=jnp.float32) * score_scale
            scores = jnp.where(causal, scores, masked_score)
            largest = lax.optimization_barrier(jnp.max(scores, axis=1, keepdims=True))
            weights = jnp.where(causal, jnp.exp(scores - largest), 0.0)
            totals = lax.optimization_barrier(jnp.sum(weights, axis=1, keepdims=True))
            mixed = jnp.dot(weights.astype(jnp.bfloat16), value_head, preferred_element_type=jnp.float32)
            return (mixed / totals).astype(jnp.bfloat16)
        return lax.map(one_block, (query_head, query_pos)).reshape(KEPT_ROW_TOTAL, HEAD_SIZE)
    heads_out = lax.map(one_head, jnp.arange(QUERY_HEADS, dtype=jnp.int32))
    return heads_out.transpose(1, 0, 2).reshape(KEPT_ROW_TOTAL, QUERY_HEADS * HEAD_SIZE)
```

```python
import math

import jax
import jax.numpy as jnp
from jax import lax
from jax.experimental import pallas as pl
from jax.experimental.pallas import tpu as pltpu
from jax.sharding import PartitionSpec as P

HEAD_SIZE = 128
QUERY_HEADS = 32
KEY_VALUE_HEADS = 4
ROWS_DEV = 128
CAP = 384
N_CTX = 32
N_TP = 16
MESH = pl.DeviceIdType.MESH
rope_base = 500000.0
masked_score = -1e30
BF16 = jnp.bfloat16
F32 = jnp.float32


def iota(shape, dim):
    return lax.broadcasted_iota(jnp.int32, shape, dim)


def kernel(info_ref, inv_ref, hidden_hbm, wq_hbm, kvw_hbm, out_ref,
           info_all, hidden, kvw, outb, inb, xall, wall, kvpart, kvin, kvall, trig, qbuf,
           load_sem, send_sem, info_sem, a2a_sem, w_sem, w_sib, x_sem, rs_sem, kv_sem):
    c = lax.axis_index("ctx")
    t = lax.axis_index("tp")
    xh, z, co = c // 16, lax.rem(c // 2, 8), lax.rem(c, 2)
    y, xl = t // 2, lax.rem(t, 2)
    idx = c // 2
    m = lax.rem(t, 4)

    def ctx_of(h, zz, cc):
        return {"ctx": (h * 8 + zz) * 2 + cc}

    z_right, z_left = ctx_of(xh, lax.rem(z + 1, 8), co), ctx_of(xh, lax.rem(z + 7, 8), co)
    sibling, far_x = ctx_of(xh, z, 1 - co), ctx_of(1 - xh, z, co)
    y_right, y_left = {"tp": lax.rem(y + 1, 8) * 2 + xl}, {"tp": lax.rem(y + 7, 8) * 2 + xl}
    near_x = {"tp": y * 2 + 1 - xl}
    y_pair = {"tp": (y + 1 - 2 * lax.rem(y, 2)) * 2 + xl}

    def send(src, dst, ss, rs, device):
        pltpu.make_async_remote_copy(
            src_ref=src, dst_ref=dst, send_sem=ss, recv_sem=rs, device_id=device, device_id_type=MESH
        ).start()

    def wait(ref, sem):
        pltpu.make_async_copy(ref, ref, sem).wait()

    barrier = pltpu.get_barrier_semaphore()

    @pl.loop(1, N_CTX)
    def _(d):
        pl.semaphore_signal(barrier, inc=1, device_id={"ctx": lax.rem(c + d, N_CTX)}, device_id_type=MESH)

    @pl.loop(1, N_TP)
    def _(d):
        pl.semaphore_signal(barrier, inc=1, device_id={"tp": lax.rem(t + d, N_TP)}, device_id_type=MESH)

    loads = [
        pltpu.make_async_copy(wq_hbm, wall.at[c], load_sem.at[0]),
        pltpu.make_async_copy(hidden_hbm, hidden, load_sem.at[1]),
        pltpu.make_async_copy(kvw_hbm, kvw, load_sem.at[2]),
    ]
    for load in loads:
        load.start()
    info_all[c] = info_ref[...]
    loads[0].wait()
    pl.semaphore_wait(barrier, N_CTX + N_TP - 2)

    @pl.loop(1, N_CTX)
    def _(d):
        send(info_ref, info_all.at[c], send_sem.at[0], info_sem.at[0], {"ctx": lax.rem(c + d, N_CTX)})

    halves = (xh, 1 - xh)

    def w_block(r, zz, cc):
        return wall.at[(halves[r] * 8 + zz) * 2 + cc]

    def w_send(r, zz, device, sem):
        block = w_block(r, zz, co)
        send(block, block, send_sem.at[1], sem, device)

    w_right = (4, 3)

    def w_start(r):
        w_send(r, z, z_right, w_sem.at[r * 8])
        w_send(r, z, z_left, w_sem.at[r * 8 + 4])
        w_send(r, z, sibling, w_sib.at[0])

    def w_step(s):
        for r in range(2):
            if s < w_right[r]:
                zz = lax.rem(z + 7 - s, 8)
                wait(w_block(r, zz, co), w_sem.at[r * 8 + s])
                if s + 1 < w_right[r]:
                    w_send(r, zz, z_right, w_sem.at[r * 8 + s + 1])
                w_send(r, zz, sibling, w_sib.at[0])
            if s < 7 - w_right[r]:
                zz = lax.rem(z + 1 + s, 8)
                wait(w_block(r, zz, co), w_sem.at[r * 8 + 4 + s])
                if s + 1 < 7 - w_right[r]:
                    w_send(r, zz, z_left, w_sem.at[r * 8 + 4 + s + 1])
                w_send(r, zz, sibling, w_sib.at[0])

    w_send(0, z, far_x, w_sem.at[16])
    w_start(0)

    wait(info_all.at[pl.ds(0, N_CTX - 1)], info_sem.at[0])
    counts = info_all[:, 3, :]
    shard = iota((N_CTX, 128), 0)
    own_offset = jnp.sum(jnp.where(shard < c, counts, 0), axis=0, keepdims=True)
    counts_wide = jnp.concatenate([counts] * 4, axis=1)
    shard_wide, column = iota((N_CTX, 512), 0), iota((N_CTX, 512), 1)
    first = jnp.sum(jnp.where(shard_wide < column // 16, counts_wide, 0), axis=0, keepdims=True)
    number = jnp.sum(jnp.where(shard_wide == column // 16, counts_wide, 0), axis=0, keepdims=True)
    lane = iota((N_CTX, 128), 1)
    first_of = jnp.sum(jnp.where(shard < lane, counts, 0), axis=0, keepdims=True)
    number_of = jnp.sum(jnp.where(shard == lane, counts, 0), axis=0, keepdims=True)

    slot = iota((1, CAP), 1)
    place = ((slot + jnp.concatenate([own_offset] * 3, axis=1)) % 32) * 16 + slot // 32
    loads[1].wait()
    for part in range(4):
        chosen = (iota((128, CAP), 0) + 128 * part == place).astype(F32).astype(BF16)
        outb[pl.ds(part * 128, 128)] = jnp.dot(chosen, hidden[...], preferred_element_type=F32).astype(BF16)
    mine = pl.ds(pl.multiple_of(c * 16, 16), 16)
    inb[mine] = outb[mine]

    @pl.loop(1, N_CTX)
    def _(d):
        peer = lax.rem(c + d, N_CTX)
        send(outb.at[pl.ds(pl.multiple_of(peer * 16, 16), 16)], inb.at[mine], send_sem.at[2], a2a_sem.at[0], {"ctx": peer})

    rank = iota((ROWS_DEV, 128), 0) * N_CTX + c
    from_shard = (rank >= first_of) & (rank < first_of + number_of)
    within = jnp.sum(jnp.where(from_shard, rank - first_of, 0).astype(F32), axis=1, keepdims=True)
    source = from_shard.astype(F32).astype(BF16)[:, :N_CTX]
    picked = jnp.zeros((ROWS_DEV, 128), F32)
    for part in range(3):
        place_of = info_all[:, part, :]
        high = jnp.dot(source, (place_of // 256).astype(F32).astype(BF16), preferred_element_type=F32)
        low = jnp.dot(source, (place_of % 256).astype(F32).astype(BF16), preferred_element_type=F32)
        here = iota((ROWS_DEV, 128), 1).astype(F32) + 128.0 * part == within
        picked += jnp.where(here, high * 256.0 + low, 0.0)
    angles = jnp.sum(picked, axis=1, keepdims=True) * inv_ref[0:1, :]
    trig[0] = jnp.cos(angles)
    trig[1] = jnp.where(iota((ROWS_DEV, 128), 1) < HEAD_SIZE // 2, -1.0, 1.0) * jnp.sin(angles)

    def rotate(u, cosine, sine):
        return u * cosine + pltpu.roll(u, HEAD_SIZE // 2, 1) * sine

    pick_rank = iota((ROWS_DEV, 512), 0) * N_CTX + c
    low_rank = first + 32 * (iota((1, 512), 1) % 16)
    high_rank = jnp.minimum(low_rank + 32, first + number)
    pick = ((pick_rank >= low_rank) & (pick_rank < high_rank)).astype(F32).astype(BF16)
    wait(inb.at[pl.ds(0, 16 * (N_CTX - 1))], a2a_sem.at[0])
    rows = jnp.dot(pick, inb[...], preferred_element_type=F32).astype(BF16)
    xall[t] = rows

    sides = (xl, 1 - xl)
    x_right = (4, 3)

    def x_block(r, yy):
        return xall.at[yy * 2 + sides[r]]

    def x_send(r, yy, device, sem):
        block = x_block(r, yy)
        send(block, block, send_sem.at[3], sem, device)

    def x_start(r):
        x_send(r, y, y_right, x_sem.at[r * 8])
        x_send(r, y, y_left, x_sem.at[r * 8 + 4])

    def x_step(s):
        for r in range(2):
            if s < x_right[r]:
                yy = lax.rem(y + 7 - s, 8)
                wait(x_block(r, yy), x_sem.at[r * 8 + s])
                if s + 1 < x_right[r]:
                    x_send(r, yy, y_right, x_sem.at[r * 8 + s + 1])
            if s < 7 - x_right[r]:
                yy = lax.rem(y + 1 + s, 8)
                wait(x_block(r, yy), x_sem.at[r * 8 + 4 + s])
                if s + 1 < 7 - x_right[r]:
                    x_send(r, yy, y_left, x_sem.at[r * 8 + 4 + s + 1])

    x_send(0, y, near_x, x_sem.at[16])
    x_start(0)

    loads[2].wait()
    for g in range(KEY_VALUE_HEADS):
        kvpart[g] = jnp.dot(rows, kvw[:, g * 256:(g + 1) * 256], preferred_element_type=F32).astype(BF16)

    @pl.loop(1, N_TP)
    def _(d):
        peer = lax.rem(t + d, N_TP)
        send(kvpart.at[peer // 4, pl.ds(pl.multiple_of(lax.rem(peer, 4) * 32, 32), 32)], kvin.at[t],
             send_sem.at[4], rs_sem.at[0], {"tp": peer})

    mine_kv = pl.ds(pl.multiple_of(m * 32, 32), 32)
    kvin[t] = kvpart[t // 4, mine_kv]
    wait(x_block(1, y), x_sem.at[16])
    x_start(1)
    wait(w_block(1, z, co), w_sem.at[16])
    w_start(1)
    w_step(0)
    x_step(0)
    w_step(1)

    wait(kvin.at[pl.ds(0, N_TP - 1)], rs_sem.at[0])
    total = jnp.zeros((32, 256), F32)
    for s in range(N_TP):
        total += kvin[s].astype(F32)
    kvall[m, co, idx, :, :HEAD_SIZE] = rotate(total[:, :HEAD_SIZE], trig[0, mine_kv], trig[1, mine_kv]).astype(BF16)
    kvall[m, co, idx, :, HEAD_SIZE:] = total[:, HEAD_SIZE:].astype(BF16)

    @pl.loop(1, 16)
    def _(d):
        block = kvall.at[m, co, idx]
        send(block, block, send_sem.at[5], kv_sem.at[0], {"ctx": lax.rem(idx + d, 16) * 2 + co})

    x_step(1)
    w_step(2)
    x_step(2)
    w_step(3)
    wait(kvall.at[m, co, pl.ds(0, 15)], kv_sem.at[0])

    def kv_send(ref, device, sem):
        send(ref, ref, send_sem.at[6], sem, device)

    mx, my, mxy = m + 1 - 2 * xl, lax.rem(m + 2, 4), 3 - m
    kv_send(kvall.at[m, co], near_x, kv_sem.at[1])
    kv_send(kvall.at[m, co], y_pair, kv_sem.at[2])
    kv_send(kvall.at[m, co], sibling, kv_sem.at[5])
    x_step(3)
    lo_half, hi_half = pl.ds(0, 8), pl.ds(8, 8)
    wait(kvall.at[mx, co], kv_sem.at[1])
    kv_send(kvall.at[mx, co, lo_half], y_pair, kv_sem.at[3])
    kv_send(kvall.at[mx, co], sibling, kv_sem.at[6])
    wait(kvall.at[my, co], kv_sem.at[2])
    kv_send(kvall.at[my, co, hi_half], near_x, kv_sem.at[4])
    kv_send(kvall.at[my, co], sibling, kv_sem.at[7])

    wait(wall.at[pl.ds(0, 16)], w_sib.at[0])

    def add_block(k, acc):
        weight = wall[pl.ds(k * 2, 2)].reshape(512, 256)
        return acc + jnp.dot(xall[k], weight, preferred_element_type=F32)

    q = lax.fori_loop(0, N_TP, add_block, jnp.zeros((ROWS_DEV, 256), F32))
    for head in range(2):
        turned = rotate(q[:, head * 128:(head + 1) * 128], trig[0], trig[1]).astype(BF16)
        for j in range(4):
            qbuf[j, head * 32:(head + 1) * 32, :] = turned[j * 32:(j + 1) * 32]

    wait(kvall.at[mxy, co, lo_half], kv_sem.at[3])
    wait(kvall.at[mxy, co, hi_half], kv_sem.at[4])
    kv_send(kvall.at[mxy, co], sibling, kv_sem.at[8])
    wait(kvall.at[m, 1 - co], kv_sem.at[5])
    wait(kvall.at[mx, 1 - co], kv_sem.at[6])
    wait(kvall.at[my, 1 - co], kv_sem.at[7])
    wait(kvall.at[mxy, 1 - co], kv_sem.at[8])

    scale = 1.0 / math.sqrt(HEAD_SIZE)
    key_index = iota((64, 1024), 1)
    query_row = iota((64, 1024), 0) % 32
    key_row = key_index % 32
    key_ctx = (key_index // 32 % 16) * 2 + key_index // 512
    seen = (key_row < query_row) | ((key_row == query_row) & (key_ctx <= c))
    for j in range(4):
        scores = []
        for b in range(j + 1):
            keys = kvall[b, :, :, :, :HEAD_SIZE].reshape(1024, HEAD_SIZE)
            part = lax.dot_general(qbuf[j], keys, (((1,), (1,)), ((), ())), preferred_element_type=F32) * scale
            scores.append(jnp.where(seen, part, masked_score) if b == j else part)
        largest = jnp.max(scores[0], axis=1, keepdims=True)
        for part in scores[1:]:
            largest = jnp.maximum(largest, jnp.max(part, axis=1, keepdims=True))
        sums = jnp.zeros((64, 1), F32)
        mixed = jnp.zeros((64, HEAD_SIZE), F32)
        for b in range(j + 1):
            weights = jnp.exp(scores[b] - largest)
            if b == j:
                weights = jnp.where(seen, weights, 0.0)
            sums += jnp.sum(weights, axis=1, keepdims=True)
            values = kvall[b, :, :, :, HEAD_SIZE:].reshape(1024, HEAD_SIZE)
            mixed += jnp.dot(weights.astype(BF16), values, preferred_element_type=F32)
        result = (mixed / sums).astype(BF16)
        for head in range(2):
            out_ref[j * 32:(j + 1) * 32, head * 128:(head + 1) * 128] = result[head * 32:(head + 1) * 32]

    wait(info_all.at[pl.ds(0, N_CTX - 1)], send_sem.at[0])
    wait(wall.at[pl.ds(0, 16)], send_sem.at[1])
    wait(wall.at[pl.ds(0, 15)], send_sem.at[1])
    wait(outb.at[pl.ds(0, 16 * (N_CTX - 1))], send_sem.at[2])
    wait(xall.at[pl.ds(0, 15)], send_sem.at[3])
    wait(kvin.at[pl.ds(0, N_TP - 1)], send_sem.at[4])
    wait(kvall.at[m, co, pl.ds(0, 15)], send_sem.at[5])
    wait(kvall.at[pl.ds(0, 3)], send_sem.at[6])
    wait(kvall.at[m, co, pl.ds(0, 8)], send_sem.at[6])
    wait(kvall.at[m, co, pl.ds(0, 8)], send_sem.at[6])


def on_device(hidden, counts, positions, w_query, key_value_weight):
    info = jnp.concatenate(
        [positions.reshape(3, 128), jnp.broadcast_to(counts[:, None], (1, 128)), jnp.zeros((4, 128), jnp.int32)], axis=0
    )
    half = HEAD_SIZE // 2
    exponent = jnp.arange(half, dtype=F32) * (2.0 / HEAD_SIZE)
    inverse = jnp.power(jnp.float32(rope_base), -exponent)
    inverse = jnp.broadcast_to(jnp.concatenate([inverse, inverse])[None, :], (8, 128))
    vmem, anywhere = pl.BlockSpec(memory_space=pltpu.VMEM), pl.BlockSpec(memory_space=pl.ANY)
    dma = pltpu.SemaphoreType.DMA
    return pl.pallas_call(
        kernel,
        out_shape=jax.ShapeDtypeStruct((ROWS_DEV, 256), BF16),
        in_specs=[vmem, vmem, anywhere, anywhere, anywhere],
        out_specs=vmem,
        scratch_shapes=[
            pltpu.VMEM((N_CTX, 8, 128), jnp.int32),
            pltpu.VMEM((CAP, 512), BF16),
            pltpu.VMEM((512, 1024), BF16),
            pltpu.VMEM((512, 512), BF16),
            pltpu.VMEM((512, 512), BF16),
            pltpu.VMEM((N_TP, ROWS_DEV, 512), BF16),
            pltpu.VMEM((N_CTX, 256, 256), BF16),
            pltpu.VMEM((4, ROWS_DEV, 256), BF16),
            pltpu.VMEM((N_TP, 32, 256), BF16),
            pltpu.VMEM((4, 2, 16, 32, 256), BF16),
            pltpu.VMEM((2, ROWS_DEV, 128), F32),
            pltpu.VMEM((4, 64, 128), BF16),
            dma((3,)),
            dma((7,)),
            dma((1,)),
            dma((1,)),
            dma((17,)),
            dma((1,)),
            dma((17,)),
            dma((1,)),
            dma((9,)),
        ],
        compiler_params=pltpu.CompilerParams(
            collective_id=0, has_side_effects=True, vmem_limit_bytes=48 * 1024 * 1024
        ),
        name="gqa",
    )(info, inverse, hidden, w_query, key_value_weight)


def solution(mesh):
    return jax.shard_map(
        on_device,
        mesh=mesh,
        in_specs=(P("ctx", "tp"), P("ctx"), P("ctx"), P("ctx", "tp"), P("tp", None)),
        out_specs=P("ctx", "tp"),
        check_vma=False,
    )
```

```python
import math

import jax
import jax.numpy as jnp
import numpy as np
from jax import lax
from jax.experimental import pallas as pl
from jax.experimental.pallas import tpu as pltpu
from jax.sharding import PartitionSpec as P

HEAD_SIZE = 128
QUERY_HEADS = 32
KEY_VALUE_HEADS = 4
ROWS_DEV = 128
CAP = 384
N_CTX = 32
N_TP = 16
MESH = pl.DeviceIdType.MESH
rope_base = 500000.0
masked_score = -1e30
BF16 = jnp.bfloat16
F32 = jnp.float32


def iota(shape, dim):
    return lax.broadcasted_iota(jnp.int32, shape, dim)


def kernel(counts_ref, inv_hbm, pos_hbm, hidden_hbm, wq_hbm, kvw_hbm, out_ref,
           counts_all, pos_all, inv_ref, hidden, kvw, wq, outb, inb, xall, wall, kvfull, kvp, kvx, kvs, kvin, kvall,
           trig, qpart, qin, qbuf,
           load_sem, send_sem, info_sem, pos_sem, a2a_sem, w_sem, w_far, w_sib, x_sem, rs_sem, kv_sem, q_sem):
    c = lax.axis_index("ctx")
    t = lax.axis_index("tp")
    xh, z, co = c // 16, lax.rem(c // 2, 8), lax.rem(c, 2)
    y, xl = t // 2, lax.rem(t, 2)
    idx = c // 2
    m = lax.rem(t, 4)

    def ctx_of(h, zz, cc):
        return {"ctx": (h * 8 + zz) * 2 + cc}

    z_near = (ctx_of(xh, lax.rem(z + 1, 8), co), ctx_of(xh, lax.rem(z + 7, 8), co))
    sibling, far_x = ctx_of(xh, z, 1 - co), ctx_of(1 - xh, z, co)
    y_right, y_left = {"tp": lax.rem(y + 1, 8) * 2 + xl}, {"tp": lax.rem(y + 7, 8) * 2 + xl}
    near_x = {"tp": y * 2 + 1 - xl}
    y_pair = {"tp": (y + 1 - 2 * lax.rem(y, 2)) * 2 + xl}

    def send(src, dst, ss, rs, device):
        pltpu.make_async_remote_copy(
            src_ref=src, dst_ref=dst, send_sem=ss, recv_sem=rs, device_id=device, device_id_type=MESH
        ).start()

    def wait(ref, sem):
        pltpu.make_async_copy(ref, ref, sem).wait()

    barrier = pltpu.get_barrier_semaphore()

    @pl.loop(1, N_CTX)
    def _(d):
        pl.semaphore_signal(barrier, inc=1, device_id={"ctx": lax.rem(c + d, N_CTX)}, device_id_type=MESH)

    @pl.loop(1, N_TP)
    def _(d):
        pl.semaphore_signal(barrier, inc=1, device_id={"tp": lax.rem(t + d, N_TP)}, device_id_type=MESH)

    loads = [
        pltpu.make_async_copy(wq_hbm, wq, load_sem.at[0]),
        pltpu.make_async_copy(hidden_hbm, hidden, load_sem.at[1]),
        pltpu.make_async_copy(kvw_hbm, kvw, load_sem.at[2]),
        pltpu.make_async_copy(pos_hbm, pos_all.at[c], load_sem.at[3]),
        pltpu.make_async_copy(inv_hbm, inv_ref, load_sem.at[4]),
    ]
    for load in loads:
        load.start()
    counts_all[c] = counts_ref[...]
    loads[0].wait()
    pl.semaphore_wait(barrier, N_CTX + N_TP - 2)

    @pl.loop(1, N_CTX)
    def _(d):
        send(counts_ref, counts_all.at[c], send_sem.at[0], info_sem.at[0], {"ctx": lax.rem(c + d, N_CTX)})

    source = lax.rem(z + xl, 2) == 0
    other = lax.rem(z + xl, 2)
    relay = other == 1
    halves, sides = (xh, 1 - xh), (xl, 1 - xl)
    one_way = {(0, 0): 0, (0, 1): 1}

    def w_block(r, jj, zz, u):
        return wall.at[halves[r] * 4 + zz // 2, sides[jj], co, pl.ds(u * 128, 128)]

    def w_send(block, device, sem):
        send(block, block, send_sem.at[1], sem, device)

    def ring_sem(r, jj, way, slot, u):
        return w_sem.at[(((r * 2 + jj) * 2 + way) * 2 + slot) * 2 + u]

    def w_start(r, jj, u):
        block = w_block(r, jj, z, u)
        for way in range(2):
            w_send(block, z_near[way], ring_sem(r, jj, way, 0, u))
        w_send(block, far_x, w_far.at[jj])
        w_send(block, sibling, w_sib.at[0])

    def from_z(way, distance):
        return lax.rem(z + 8 - distance, 8) if way == 0 else lax.rem(z + distance, 8)

    def w_slot(r, jj, way, slot, ways):
        for u in range(2):
            block = w_block(r, jj, from_z(way, 2 + 2 * slot - other), u)
            wait(block, ring_sem(r, jj, way, slot, u))
            if way in ways:
                w_send(block, z_near[way], ring_sem(r, jj, way, 1 - other if slot == 0 else 1, u))
            w_send(block, far_x, w_far.at[jj])
            w_send(block, sibling, w_sib.at[0])

    def w_first(r, jj):
        for way in range(2):
            w_slot(r, jj, way, 0, (0, 1))

    def w_first_if(condition, r, jj):
        @pl.when(condition)
        def _():
            w_first(r, jj)

    def w_second_if(condition, r, jj):
        @pl.when(condition)
        def _():
            if condition is source:
                w_slot(r, jj, one_way[r, jj], 1, ())
            else:
                for way in range(2):
                    w_slot(r, jj, way, 1, (one_way[r, jj],))

    def w_second(r, jj):
        @pl.when(source)
        def _():
            w_slot(r, jj, one_way[r, jj], 1, ())

        @pl.when(jnp.logical_not(source))
        def _():
            for way in range(2):
                w_slot(r, jj, way, 1, (one_way[r, jj],))

    @pl.when(source)
    def _():
        wall[xh * 4 + z // 2, xl, co] = wq[...]
        for u in range(2):
            w_start(0, 0, u)
        for u in range(2):
            wait(w_block(0, 1, z, u), w_sem.at[32 + u])
            w_start(0, 1, u)
        w_first(0, 0)

    @pl.when(jnp.logical_not(source))
    def _():
        for u in range(2):
            rows_u = pl.ds(u * 128, 128)
            send(wq.at[rows_u], wall.at[xh * 4 + z // 2, xl, co, rows_u], send_sem.at[1], w_sem.at[32 + u], near_x)
        w_first(0, 0)
        w_first(0, 1)

    loads[3].wait()

    @pl.loop(1, N_CTX)
    def _(d):
        send(pos_all.at[c], pos_all.at[c], send_sem.at[8], pos_sem.at[0], {"ctx": lax.rem(c + d, N_CTX)})

    wait(counts_all.at[pl.ds(0, N_CTX - 1)], info_sem.at[0])
    counts = counts_all[...].reshape(N_CTX, 128)
    shard = iota((N_CTX, 128), 0)
    own_offset = jnp.sum(jnp.where(shard < c, counts, 0), axis=0, keepdims=True)
    slot = iota((1, CAP), 1)
    place = ((slot + jnp.concatenate([own_offset] * 3, axis=1)) % 32) * 16 + slot // 32
    loads[1].wait()
    for part in range(4):
        chosen = (iota((128, CAP), 0) + 128 * part == place).astype(F32).astype(BF16)
        moved = jnp.dot(chosen, hidden[...], preferred_element_type=F32).reshape(8, 16, 512)
        for k in range(4):
            tall = moved[:, :12, k * 128:(k + 1) * 128]
            outb[pl.ds(part * 8, 8), k * 12:(k + 1) * 12, :] = tall.astype(BF16)
    inb[c] = outb[c]

    @pl.loop(1, N_CTX)
    def _(d):
        peer = lax.rem(c + d, N_CTX)
        send(outb.at[peer], inb.at[c], send_sem.at[2], a2a_sem.at[0], {"ctx": peer})

    column = iota((1, 1536), 1)
    column_shard = (column * 1366) >> 16
    in_shard = column - column_shard * 48
    column_part = (in_shard * 5462) >> 16
    column_turn = in_shard - column_part * 12
    counts_wide = jnp.concatenate([counts] * 12, axis=1)
    shard_wide = iota((N_CTX, 1536), 0)
    first = jnp.sum(jnp.where(shard_wide < column_shard, counts_wide, 0), axis=0, keepdims=True)
    number = jnp.sum(jnp.where(shard_wide == column_shard, counts_wide, 0), axis=0, keepdims=True)
    low_rank = first + 32 * column_turn
    high_rank = jnp.minimum(low_rank + 32, first + number)
    pick_rank = iota((ROWS_DEV, 1536), 0) * N_CTX + c
    pick = (pick_rank >= low_rank) & (pick_rank < high_rank)
    loads[4].wait()
    wait(pos_all.at[pl.ds(0, N_CTX - 1)], pos_sem.at[0])
    lane = iota((N_CTX, 128), 1)
    first_of = jnp.sum(jnp.where(shard < lane, counts, 0), axis=0, keepdims=True)
    number_of = jnp.sum(jnp.where(shard == lane, counts, 0), axis=0, keepdims=True)
    rank = iota((ROWS_DEV, 128), 0) * N_CTX + c
    from_shard = (rank >= first_of) & (rank < first_of + number_of)
    within = jnp.sum(jnp.where(from_shard, rank - first_of, 0).astype(F32), axis=1, keepdims=True)
    holder = from_shard.astype(F32).astype(BF16)[:, :N_CTX]
    picked = jnp.zeros((ROWS_DEV, 128), F32)
    for part in range(3):
        place_of = pos_all[:, part, :]
        high = jnp.dot(holder, (place_of // 256).astype(F32).astype(BF16), preferred_element_type=F32)
        low = jnp.dot(holder, (place_of % 256).astype(F32).astype(BF16), preferred_element_type=F32)
        here = iota((ROWS_DEV, 128), 1).astype(F32) + 128.0 * part == within
        picked += jnp.where(here, high * 256.0 + low, 0.0)
    angles = jnp.sum(picked, axis=1, keepdims=True) * inv_ref[0:1, :]
    trig[0] = jnp.cos(angles)
    trig[1] = jnp.where(iota((ROWS_DEV, 128), 1) < HEAD_SIZE // 2, -1.0, 1.0) * jnp.sin(angles)

    wait(inb.at[pl.ds(0, N_CTX - 1)], a2a_sem.at[0])
    arrived = inb[...].reshape(1536, 128)
    for k in range(4):
        chosen = (pick & (column_part == k)).astype(F32).astype(BF16)
        xall[y, :, k * 128:(k + 1) * 128] = jnp.dot(chosen, arrived, preferred_element_type=F32).astype(BF16)

    def x_send(ref, device, sem):
        send(ref, ref, send_sem.at[3], sem, device)

    def x_part(yy, u):
        return xall.at[yy, pl.ds(u * 64, 64)]

    for u in range(2):
        x_send(x_part(y, u), y_right, x_sem.at[u])
        x_send(x_part(y, u), y_left, x_sem.at[8 + u])

    def x_step(s):
        for u in range(2):
            for way, device in ((0, y_right), (1, y_left)):
                if s == 3 and u != way:
                    continue
                part = x_part(lax.rem(y + (7 - s if way == 0 else 1 + s), 8), u)
                wait(part, x_sem.at[way * 8 + s * 2 + u])
                if s < 2 or (s == 2 and u == way):
                    x_send(part, device, x_sem.at[way * 8 + (s + 1) * 2 + u])

    loads[2].wait()
    rows = xall[y]
    for g in range(KEY_VALUE_HEADS):
        partial = jnp.dot(rows, kvw[:, g * 256:(g + 1) * 256], preferred_element_type=F32)
        for quarter in range(4):
            piece = partial[quarter * 32:(quarter + 1) * 32]
            kvfull[quarter % 2, g * 2 + quarter // 2] = piece
            kvp[quarter % 2, g * 2 + quarter // 2] = piece.astype(BF16)
    send(kvp.at[1 - xl], kvx, send_sem.at[4], rs_sem.at[0], near_x)

    def rotate(u, cosine, sine):
        return u * cosine + pltpu.roll(u, HEAD_SIZE // 2, 1) * sine

    own_kv = kvall.at[m, co, idx]
    z_half = z // 4

    def kv_where(n):
        return halves[n // 2], z_half if n % 2 == 0 else 1 - z_half

    def kv_send(ref, device, sem):
        send(ref, ref, send_sem.at[7], sem, device)

    mx, my, mxy = m + 1 - 2 * xl, lax.rem(m + 2, 4), 3 - m

    def kv_chunk(b, n):
        hh, half_z = kv_where(n)
        return kvall.at[b, co, pl.ds(pl.multiple_of(hh * 8 + half_z * 4, 4), 4)]

    def kv_out(n):
        wait(kvall.at[m, co, pl.ds(0, 4 if n else 3)], kv_sem.at[n])
        block = kv_chunk(m, n)
        kv_send(block, y_pair, kv_sem.at[4 + n])
        kv_send(block, near_x, kv_sem.at[8 + n])
        kv_send(block, sibling, kv_sem.at[16])

    def kv_mid(n):
        block = kv_chunk(mx if n % 2 else my, n)
        wait(block, kv_sem.at[8 + n if n % 2 else 4 + n])
        kv_send(block, y_pair if n % 2 else near_x, kv_sem.at[12 + n])
        kv_send(block, sibling, kv_sem.at[16])

    def kv_last(n):
        for block, k in ((kv_chunk(my if n % 2 else mx, n), 4 + n if n % 2 else 8 + n), (kv_chunk(mxy, n), 12 + n)):
            wait(block, kv_sem.at[k])
            kv_send(block, sibling, kv_sem.at[16])

    def partial_queries(j):
        def add_block(k, acc):
            return acc + jnp.dot(xall[k], wall[k, j].reshape(512, 256), preferred_element_type=F32)

        return lax.fori_loop(0, 8, add_block, jnp.zeros((ROWS_DEV, 256), F32))

    w_first_if(source, 0, 1)
    w_second(0, 0)
    wait(kvx, rs_sem.at[0])
    kvs[...] = (kvfull[xl] + kvx[...].astype(F32)).astype(BF16)
    kvin[y] = kvs[y]

    @pl.loop(1, 8)
    def _(d):
        peer = lax.rem(y + d, 8)
        send(kvs.at[peer], kvin.at[y], send_sem.at[5], rs_sem.at[1], {"tp": peer * 2 + xl})

    x_step(0)
    w_second(0, 1)
    x_step(1)
    mine_kv = pl.ds(pl.multiple_of(m * 32, 32), 32)
    wait(kvin.at[pl.ds(0, 7)], rs_sem.at[1])
    total = jnp.zeros((32, 256), F32)
    for s in range(8):
        total += kvin[s].astype(F32)
    kvall[m, co, idx, :, :HEAD_SIZE] = rotate(total[:, :HEAD_SIZE], trig[0, mine_kv], trig[1, mine_kv]).astype(BF16)
    kvall[m, co, idx, :, HEAD_SIZE:] = total[:, HEAD_SIZE:].astype(BF16)

    for n in range(4):
        hh, half_z = kv_where(n)

        @pl.loop(1 if n == 0 else 0, 4)
        def _(d):
            send(own_kv, own_kv, send_sem.at[6], kv_sem.at[n], ctx_of(hh, half_z * 4 + lax.rem(z + d, 4), co))

    x_step(2)
    kv_out(0)
    kv_out(1)
    kv_mid(0)
    wait(wall.at[pl.ds(0, 1)], w_far.at[0])
    w_send(wall.at[pl.ds((1 - xh) * 4, 4), sides[0], co], sibling, w_sib.at[0])
    wait(wall.at[pl.ds(0, 1)], w_far.at[1])
    w_send(wall.at[pl.ds((1 - xh) * 4, 4), sides[1], co], sibling, w_sib.at[0])
    kv_out(2)
    kv_mid(1)
    kv_out(3)
    x_step(3)
    kv_mid(2)
    wait(wall.at[pl.ds(0, 4)], w_sib.at[0])
    qpart[...] = partial_queries(1 - xl).astype(BF16)
    send(qpart, qin, send_sem.at[9], q_sem.at[0], near_x)
    kv_last(0)
    kv_mid(3)
    kv_last(1)
    q = partial_queries(xl)
    kv_last(2)
    kv_last(3)
    wait(qin, q_sem.at[0])
    q = q + qin[...].astype(F32)
    for head in range(2):
        turned = rotate(q[:, head * 128:(head + 1) * 128], trig[0], trig[1]).astype(BF16)
        for j in range(4):
            qbuf[j, head * 32:(head + 1) * 32, :] = turned[j * 32:(j + 1) * 32]

    wait(kvall.at[pl.ds(0, 2)], kv_sem.at[16])

    scale = 1.0 / math.sqrt(HEAD_SIZE)
    key_index = iota((64, 1024), 1)
    query_row = iota((64, 1024), 0) % 32
    key_row = key_index % 32
    key_ctx = (key_index // 32 % 16) * 2 + key_index // 512
    seen = (key_row < query_row) | ((key_row == query_row) & (key_ctx <= c))
    for j in range(4):
        scores = []
        for b in range(j + 1):
            keys = kvall[b, :, :, :, :HEAD_SIZE].reshape(1024, HEAD_SIZE)
            part = lax.dot_general(qbuf[j], keys, (((1,), (1,)), ((), ())), preferred_element_type=F32) * scale
            scores.append(jnp.where(seen, part, masked_score) if b == j else part)
        largest = jnp.max(scores[0], axis=1, keepdims=True)
        for part in scores[1:]:
            largest = jnp.maximum(largest, jnp.max(part, axis=1, keepdims=True))
        sums = jnp.zeros((64, 1), F32)
        mixed = jnp.zeros((64, HEAD_SIZE), F32)
        for b in range(j + 1):
            weights = jnp.exp(scores[b] - largest)
            if b == j:
                weights = jnp.where(seen, weights, 0.0)
            sums += jnp.sum(weights, axis=1, keepdims=True)
            values = kvall[b, :, :, :, HEAD_SIZE:].reshape(1024, HEAD_SIZE)
            mixed += jnp.dot(weights.astype(BF16), values, preferred_element_type=F32)
        result = (mixed / sums).astype(BF16)
        for head in range(2):
            out_ref[j * 32:(j + 1) * 32, head * 128:(head + 1) * 128] = result[head * 32:(head + 1) * 32]

    wait(counts_all.at[pl.ds(0, N_CTX - 1)], send_sem.at[0])

    @pl.when(source)
    def _():
        wait(wall, send_sem.at[1])

    @pl.when(jnp.logical_not(source))
    def _():
        wait(wall.at[pl.ds(0, 7)], send_sem.at[1])
        wait(wall.at[0, pl.ds(0, 1)], send_sem.at[1])
        wait(wq, send_sem.at[1])

    wait(inb.at[pl.ds(0, N_CTX - 1)], send_sem.at[2])
    wait(xall.at[pl.ds(0, 7)], send_sem.at[3])
    wait(kvx, send_sem.at[4])
    wait(kvin.at[pl.ds(0, 7)], send_sem.at[5])
    wait(kvall.at[m, co, pl.ds(0, 15)], send_sem.at[6])
    wait(kvall.at[pl.ds(0, 3)], send_sem.at[7])
    wait(kvall.at[m, co], send_sem.at[7])
    wait(pos_all.at[pl.ds(0, N_CTX - 1)], send_sem.at[8])
    wait(qin, send_sem.at[9])


def on_device(hidden, counts, positions, w_query, key_value_weight):
    exponent = np.arange(HEAD_SIZE // 2, dtype=np.float32) * np.float32(2.0 / HEAD_SIZE)
    inverse = np.power(np.float64(rope_base), -exponent.astype(np.float64)).astype(np.float32)
    inverse = jnp.asarray(np.tile(inverse, (8, 2)))
    vmem, hbm = pl.BlockSpec(memory_space=pltpu.VMEM), pl.BlockSpec(memory_space=pltpu.HBM)
    dma = pltpu.SemaphoreType.DMA
    return pl.pallas_call(
        kernel,
        out_shape=jax.ShapeDtypeStruct((ROWS_DEV, 256), BF16),
        in_specs=[vmem, hbm, hbm, hbm, hbm, hbm],
        out_specs=vmem,
        scratch_shapes=[
            pltpu.VMEM((N_CTX, 1, 128), jnp.int32),
            pltpu.VMEM((N_CTX, 3, 128), jnp.int32),
            pltpu.VMEM((8, 128), F32),
            pltpu.VMEM((CAP, 512), BF16),
            pltpu.VMEM((512, 1024), BF16),
            pltpu.VMEM((256, 256), BF16),
            pltpu.VMEM((N_CTX, 48, 128), BF16),
            pltpu.VMEM((N_CTX, 48, 128), BF16),
            pltpu.VMEM((8, ROWS_DEV, 512), BF16),
            pltpu.VMEM((8, 2, 2, 256, 256), BF16),
            pltpu.VMEM((2, 8, 32, 256), F32),
            pltpu.VMEM((2, 8, 32, 256), BF16),
            pltpu.VMEM((8, 32, 256), BF16),
            pltpu.VMEM((8, 32, 256), BF16),
            pltpu.VMEM((8, 32, 256), BF16),
            pltpu.VMEM((4, 2, 16, 32, 256), BF16),
            pltpu.VMEM((2, ROWS_DEV, 128), F32),
            pltpu.VMEM((ROWS_DEV, 256), BF16),
            pltpu.VMEM((ROWS_DEV, 256), BF16),
            pltpu.VMEM((4, 64, 128), BF16),
            dma((5,)),
            dma((10,)),
            dma((1,)),
            dma((1,)),
            dma((1,)),
            dma((34,)),
            dma((2,)),
            dma((1,)),
            dma((16,)),
            dma((2,)),
            dma((17,)),
            dma((1,)),
        ],
        compiler_params=pltpu.CompilerParams(
            collective_id=0, has_side_effects=True, vmem_limit_bytes=63 * 1024 * 1024
        ),
        name="gqa",
    )(
        jnp.broadcast_to(counts[:, None], (1, 128)), inverse, positions.reshape(3, 128),
        hidden, w_query, key_value_weight,
    )


def solution(mesh):
    return jax.shard_map(
        on_device,
        mesh=mesh,
        in_specs=(P("ctx", "tp"), P("ctx"), P("ctx"), P("ctx", "tp"), P("tp", None)),
        out_specs=P("ctx", "tp"),
        check_vma=False,
    )
```

```python
import math

import jax
import jax.numpy as jnp
import numpy as np
from jax import lax
from jax.experimental import pallas as pl
from jax.experimental.pallas import tpu as pltpu
from jax.sharding import PartitionSpec as P

HEAD_SIZE = 128
QUERY_HEADS = 32
KEY_VALUE_HEADS = 4
ROWS_DEV = 128
CAP = 384
N_CTX = 32
N_TP = 16
MESH = pl.DeviceIdType.MESH
rope_base = 500000.0
masked_score = -1e30
BF16 = jnp.bfloat16
F32 = jnp.float32


def iota(shape, dim):
    return lax.broadcasted_iota(jnp.int32, shape, dim)


def kernel(counts_ref, inv_hbm, pos_hbm, hidden_hbm, wq_hbm, kvw_hbm, out_ref,
           counts_all, pos_all, inv_ref, hidden, kvw, wq, outb, inb, xall, wall, kvfull, kvp, kvx, kvs, kvin, kvall,
           trig, qpart, qin, qbuf,
           load_sem, send_sem, info_sem, pos_sem, a2a_sem, w_sem, w_far, w_sib, x_sem, rs_sem, kv_sem, q_sem):
    c = lax.axis_index("ctx")
    t = lax.axis_index("tp")
    xh, z, co = c // 16, lax.rem(c // 2, 8), lax.rem(c, 2)
    y, xl = t // 2, lax.rem(t, 2)
    idx = c // 2
    m = lax.rem(t, 4)

    def ctx_of(h, zz, cc):
        return {"ctx": (h * 8 + zz) * 2 + cc}

    z_near = (ctx_of(xh, lax.rem(z + 1, 8), co), ctx_of(xh, lax.rem(z + 7, 8), co))
    sibling, far_x = ctx_of(xh, z, 1 - co), ctx_of(1 - xh, z, co)
    y_right, y_left = {"tp": lax.rem(y + 1, 8) * 2 + xl}, {"tp": lax.rem(y + 7, 8) * 2 + xl}
    near_x = {"tp": y * 2 + 1 - xl}
    y_pair = {"tp": (y + 1 - 2 * lax.rem(y, 2)) * 2 + xl}

    def send(src, dst, ss, rs, device):
        pltpu.make_async_remote_copy(
            src_ref=src, dst_ref=dst, send_sem=ss, recv_sem=rs, device_id=device, device_id_type=MESH
        ).start()

    def wait(ref, sem):
        pltpu.make_async_copy(ref, ref, sem).wait()

    barrier = pltpu.get_barrier_semaphore()

    @pl.loop(1, N_CTX)
    def _(d):
        pl.semaphore_signal(barrier, inc=1, device_id={"ctx": lax.rem(c + d, N_CTX)}, device_id_type=MESH)

    @pl.loop(1, N_TP)
    def _(d):
        pl.semaphore_signal(barrier, inc=1, device_id={"tp": lax.rem(t + d, N_TP)}, device_id_type=MESH)

    loads = [
        pltpu.make_async_copy(wq_hbm, wq, load_sem.at[0]),
        pltpu.make_async_copy(hidden_hbm, hidden, load_sem.at[1]),
        pltpu.make_async_copy(kvw_hbm, kvw, load_sem.at[2]),
        pltpu.make_async_copy(pos_hbm, pos_all.at[c], load_sem.at[3]),
        pltpu.make_async_copy(inv_hbm, inv_ref, load_sem.at[4]),
    ]
    for load in loads:
        load.start()
    counts_all[c] = counts_ref[...]
    loads[0].wait()
    pl.semaphore_wait(barrier, N_CTX + N_TP - 2)

    @pl.loop(1, N_CTX)
    def _(d):
        send(counts_ref, counts_all.at[c], send_sem.at[0], info_sem.at[0], {"ctx": lax.rem(c + d, N_CTX)})

    source = lax.rem(z + xl, 2) == 0
    other = lax.rem(z + xl, 2)
    relay = other == 1
    halves, sides = (xh, 1 - xh), (xl, 1 - xl)
    one_way = {(0, 0): 0, (0, 1): 1}

    def w_block(r, jj, zz, u):
        return wall.at[halves[r] * 4 + zz // 2, sides[jj], co, pl.ds(u * 128, 128)]

    def w_send(block, device, sem):
        send(block, block, send_sem.at[1], sem, device)

    def ring_sem(r, jj, way, slot, u):
        return w_sem.at[(((r * 2 + jj) * 2 + way) * 2 + slot) * 2 + u]

    def w_start(r, jj, u):
        block = w_block(r, jj, z, u)
        for way in range(2):
            w_send(block, z_near[way], ring_sem(r, jj, way, 0, u))
        w_send(block, far_x, w_far.at[jj])
        w_send(block, sibling, w_sib.at[0])

    def from_z(way, distance):
        return lax.rem(z + 8 - distance, 8) if way == 0 else lax.rem(z + distance, 8)

    def w_slot(r, jj, way, slot, ways):
        for u in range(2):
            block = w_block(r, jj, from_z(way, 2 + 2 * slot - other), u)
            wait(block, ring_sem(r, jj, way, slot, u))
            if way in ways:
                w_send(block, z_near[way], ring_sem(r, jj, way, 1 - other if slot == 0 else 1, u))
            w_send(block, far_x, w_far.at[jj])
            w_send(block, sibling, w_sib.at[0])

    def w_first(r, jj):
        for way in range(2):
            w_slot(r, jj, way, 0, (0, 1))

    def w_first_if(condition, r, jj):
        @pl.when(condition)
        def _():
            w_first(r, jj)

    def w_second_if(condition, r, jj):
        @pl.when(condition)
        def _():
            if condition is source:
                w_slot(r, jj, one_way[r, jj], 1, ())
            else:
                for way in range(2):
                    w_slot(r, jj, way, 1, (one_way[r, jj],))

    def w_second(r, jj):
        @pl.when(source)
        def _():
            w_slot(r, jj, one_way[r, jj], 1, ())

        @pl.when(jnp.logical_not(source))
        def _():
            for way in range(2):
                w_slot(r, jj, way, 1, (one_way[r, jj],))

    @pl.when(source)
    def _():
        wall[xh * 4 + z // 2, xl, co] = wq[...]
        for u in range(2):
            w_start(0, 0, u)
        for u in range(2):
            wait(w_block(0, 1, z, u), w_sem.at[32 + u])
            w_start(0, 1, u)
        w_first(0, 0)

    @pl.when(jnp.logical_not(source))
    def _():
        for u in range(2):
            rows_u = pl.ds(u * 128, 128)
            send(wq.at[rows_u], wall.at[xh * 4 + z // 2, xl, co, rows_u], send_sem.at[1], w_sem.at[32 + u], near_x)
        w_first(0, 0)
        w_first(0, 1)

    loads[3].wait()

    @pl.loop(1, N_CTX)
    def _(d):
        send(pos_all.at[c], pos_all.at[c], send_sem.at[8], pos_sem.at[0], {"ctx": lax.rem(c + d, N_CTX)})

    wait(counts_all.at[pl.ds(0, N_CTX - 1)], info_sem.at[0])
    counts = counts_all[...].reshape(N_CTX, 128)
    shard = iota((N_CTX, 128), 0)
    own_offset = jnp.sum(jnp.where(shard < c, counts, 0), axis=0, keepdims=True)
    slot = iota((1, CAP), 1)
    place = ((slot + jnp.concatenate([own_offset] * 3, axis=1)) % 32) * 16 + slot // 32
    loads[1].wait()
    for part in range(4):
        chosen = (iota((128, CAP), 0) + 128 * part == place).astype(F32).astype(BF16)
        moved = jnp.dot(chosen, hidden[...], preferred_element_type=F32).reshape(8, 16, 512)
        for k in range(4):
            tall = moved[:, :12, k * 128:(k + 1) * 128]
            outb[pl.ds(part * 8, 8), k * 12:(k + 1) * 12, :] = tall.astype(BF16)
    inb[c] = outb[c]

    @pl.loop(1, N_CTX)
    def _(d):
        peer = lax.rem(c + d, N_CTX)
        send(outb.at[peer], inb.at[c], send_sem.at[2], a2a_sem.at[0], {"ctx": peer})

    column = iota((1, 1536), 1)
    column_shard = (column * 1366) >> 16
    in_shard = column - column_shard * 48
    column_part = (in_shard * 5462) >> 16
    column_turn = in_shard - column_part * 12
    counts_wide = jnp.concatenate([counts] * 12, axis=1)
    shard_wide = iota((N_CTX, 1536), 0)
    first = jnp.sum(jnp.where(shard_wide < column_shard, counts_wide, 0), axis=0, keepdims=True)
    number = jnp.sum(jnp.where(shard_wide == column_shard, counts_wide, 0), axis=0, keepdims=True)
    low_rank = first + 32 * column_turn
    high_rank = jnp.minimum(low_rank + 32, first + number)
    pick_rank = iota((ROWS_DEV, 1536), 0) * N_CTX + c
    pick = (pick_rank >= low_rank) & (pick_rank < high_rank)
    loads[4].wait()
    wait(pos_all.at[pl.ds(0, N_CTX - 1)], pos_sem.at[0])
    lane = iota((N_CTX, 128), 1)
    first_of = jnp.sum(jnp.where(shard < lane, counts, 0), axis=0, keepdims=True)
    number_of = jnp.sum(jnp.where(shard == lane, counts, 0), axis=0, keepdims=True)
    rank = iota((ROWS_DEV, 128), 0) * N_CTX + c
    from_shard = (rank >= first_of) & (rank < first_of + number_of)
    within = jnp.sum(jnp.where(from_shard, rank - first_of, 0).astype(F32), axis=1, keepdims=True)
    holder = from_shard.astype(F32).astype(BF16)[:, :N_CTX]
    picked = jnp.zeros((ROWS_DEV, 128), F32)
    for part in range(3):
        place_of = pos_all[:, part, :]
        high = jnp.dot(holder, (place_of // 256).astype(F32).astype(BF16), preferred_element_type=F32)
        low = jnp.dot(holder, (place_of % 256).astype(F32).astype(BF16), preferred_element_type=F32)
        here = iota((ROWS_DEV, 128), 1).astype(F32) + 128.0 * part == within
        picked += jnp.where(here, high * 256.0 + low, 0.0)
    angles = jnp.sum(picked, axis=1, keepdims=True) * inv_ref[0:1, :]
    trig[0] = jnp.cos(angles)
    trig[1] = jnp.where(iota((ROWS_DEV, 128), 1) < HEAD_SIZE // 2, -1.0, 1.0) * jnp.sin(angles)

    wait(inb.at[pl.ds(0, N_CTX - 1)], a2a_sem.at[0])
    arrived = inb[...].reshape(1536, 128)
    for k in range(4):
        chosen = (pick & (column_part == k)).astype(F32).astype(BF16)
        xall[y, :, k * 128:(k + 1) * 128] = jnp.dot(chosen, arrived, preferred_element_type=F32).astype(BF16)

    def x_send(ref, device, sem):
        send(ref, ref, send_sem.at[3], sem, device)

    def x_part(yy, u):
        return xall.at[yy, pl.ds(u * 64, 64)]

    for u in range(2):
        x_send(x_part(y, u), y_right, x_sem.at[u])
        x_send(x_part(y, u), y_left, x_sem.at[8 + u])

    def x_step(s):
        for u in range(2):
            for way, device in ((0, y_right), (1, y_left)):
                if s == 3 and u != way:
                    continue
                part = x_part(lax.rem(y + (7 - s if way == 0 else 1 + s), 8), u)
                wait(part, x_sem.at[way * 8 + s * 2 + u])
                if s < 2 or (s == 2 and u == way):
                    x_send(part, device, x_sem.at[way * 8 + (s + 1) * 2 + u])

    loads[2].wait()
    rows = xall[y]
    for g in range(KEY_VALUE_HEADS):
        partial = jnp.dot(rows, kvw[:, g * 256:(g + 1) * 256], preferred_element_type=F32)
        for quarter in range(4):
            piece = partial[quarter * 32:(quarter + 1) * 32]
            kvfull[quarter % 2, g * 2 + quarter // 2] = piece
            kvp[quarter % 2, g * 2 + quarter // 2] = piece.astype(BF16)
    for h in range(2):
        part = pl.ds(h * 4, 4)
        send(kvp.at[1 - xl, part], kvx.at[part], send_sem.at[4], rs_sem.at[h], near_x)

    def rotate(u, cosine, sine):
        return u * cosine + pltpu.roll(u, HEAD_SIZE // 2, 1) * sine

    own_kv = kvall.at[m, co, idx]
    z_half = z // 4

    def kv_where(n):
        return halves[n // 2], z_half if n % 2 == 0 else 1 - z_half

    def kv_send(ref, device, sem):
        send(ref, ref, send_sem.at[7], sem, device)

    mx, my, mxy = m + 1 - 2 * xl, lax.rem(m + 2, 4), 3 - m

    def kv_chunk(b, n):
        hh, half_z = kv_where(n)
        return kvall.at[b, co, pl.ds(pl.multiple_of(hh * 8 + half_z * 4, 4), 4)]

    def kv_out(n):
        wait(kvall.at[m, co, pl.ds(0, 4 if n else 3)], kv_sem.at[n])
        block = kv_chunk(m, n)
        kv_send(block, y_pair, kv_sem.at[4 + n])
        kv_send(block, near_x, kv_sem.at[8 + n])
        kv_send(block, sibling, kv_sem.at[16])

    def kv_mid(n):
        block = kv_chunk(mx if n % 2 else my, n)
        wait(block, kv_sem.at[8 + n if n % 2 else 4 + n])
        kv_send(block, y_pair if n % 2 else near_x, kv_sem.at[12 + n])
        kv_send(block, sibling, kv_sem.at[16])

    def kv_last(n):
        for block, k in ((kv_chunk(my if n % 2 else mx, n), 4 + n if n % 2 else 8 + n), (kv_chunk(mxy, n), 12 + n)):
            wait(block, kv_sem.at[k])
            kv_send(block, sibling, kv_sem.at[16])

    def partial_queries(j):
        def add_block(k, acc):
            return acc + jnp.dot(xall[k], wall[k, j].reshape(512, 256), preferred_element_type=F32)

        return lax.fori_loop(0, 8, add_block, jnp.zeros((ROWS_DEV, 256), F32), unroll=True)

    w_first_if(source, 0, 1)
    w_second(0, 0)
    wait(kvx.at[pl.ds(0, 4)], rs_sem.at[0])
    kvs[0:4] = (kvfull[xl, 0:4] + kvx[0:4].astype(F32)).astype(BF16)

    def kvs_send(peer):
        @pl.when(peer == y)
        def _():
            kvin[y] = kvs[y]

        @pl.when(peer != y)
        def _():
            send(kvs.at[peer], kvin.at[y], send_sem.at[5], rs_sem.at[2], {"tp": peer * 2 + xl})

    @pl.loop(0, 4)
    def _(d):
        kvs_send(lax.rem(y + d, 4))

    wait(kvx.at[pl.ds(4, 4)], rs_sem.at[1])
    kvs[4:8] = (kvfull[xl, 4:8] + kvx[4:8].astype(F32)).astype(BF16)

    @pl.loop(0, 4)
    def _(d):
        kvs_send(4 + lax.rem(y + d, 4))

    x_step(0)
    w_second(0, 1)
    x_step(1)
    mine_kv = pl.ds(pl.multiple_of(m * 32, 32), 32)
    wait(kvin.at[pl.ds(0, 7)], rs_sem.at[2])
    total = jnp.zeros((32, 256), F32)
    for s in range(8):
        total += kvin[s].astype(F32)
    kvall[m, co, idx, :, :HEAD_SIZE] = rotate(total[:, :HEAD_SIZE], trig[0, mine_kv], trig[1, mine_kv]).astype(BF16)
    kvall[m, co, idx, :, HEAD_SIZE:] = total[:, HEAD_SIZE:].astype(BF16)

    for n in range(4):
        hh, half_z = kv_where(n)

        @pl.loop(1 if n == 0 else 0, 4)
        def _(d):
            send(own_kv, own_kv, send_sem.at[6], kv_sem.at[n], ctx_of(hh, half_z * 4 + lax.rem(z + d, 4), co))

    x_step(2)
    kv_out(0)
    kv_out(1)
    kv_mid(0)
    wait(wall.at[pl.ds(0, 1)], w_far.at[0])
    w_send(wall.at[pl.ds((1 - xh) * 4, 4), sides[0], co], sibling, w_sib.at[0])
    wait(wall.at[pl.ds(0, 1)], w_far.at[1])
    w_send(wall.at[pl.ds((1 - xh) * 4, 4), sides[1], co], sibling, w_sib.at[0])
    kv_out(2)
    kv_mid(1)
    kv_out(3)
    x_step(3)
    kv_mid(2)
    wait(wall.at[pl.ds(0, 4)], w_sib.at[0])
    qpart[...] = partial_queries(1 - xl).astype(BF16)
    send(qpart, qin, send_sem.at[9], q_sem.at[0], near_x)
    kv_last(0)
    kv_mid(3)
    kv_last(1)
    q = partial_queries(xl)
    kv_last(2)
    kv_last(3)
    wait(qin, q_sem.at[0])
    q = q + qin[...].astype(F32)
    for head in range(2):
        turned = rotate(q[:, head * 128:(head + 1) * 128], trig[0], trig[1]).astype(BF16)
        for j in range(4):
            qbuf[j, head * 32:(head + 1) * 32, :] = turned[j * 32:(j + 1) * 32]

    wait(kvall.at[pl.ds(0, 2)], kv_sem.at[16])

    scale = 1.0 / math.sqrt(HEAD_SIZE)
    key_index = iota((64, 1024), 1)
    query_row = iota((64, 1024), 0) % 32
    key_row = key_index % 32
    key_ctx = (key_index // 32 % 16) * 2 + key_index // 512
    seen = (key_row < query_row) | ((key_row == query_row) & (key_ctx <= c))
    for j in range(4):
        scores = []
        for b in range(j + 1):
            keys = kvall[b, :, :, :, :HEAD_SIZE].reshape(1024, HEAD_SIZE)
            part = lax.dot_general(qbuf[j], keys, (((1,), (1,)), ((), ())), preferred_element_type=F32) * scale
            scores.append(jnp.where(seen, part, masked_score) if b == j else part)
        largest = jnp.max(scores[0], axis=1, keepdims=True)
        for part in scores[1:]:
            largest = jnp.maximum(largest, jnp.max(part, axis=1, keepdims=True))
        sums = jnp.zeros((64, 1), F32)
        mixed = jnp.zeros((64, HEAD_SIZE), F32)
        for b in range(j + 1):
            weights = jnp.exp(scores[b] - largest)
            if b == j:
                weights = jnp.where(seen, weights, 0.0)
            sums += jnp.sum(weights, axis=1, keepdims=True)
            values = kvall[b, :, :, :, HEAD_SIZE:].reshape(1024, HEAD_SIZE)
            mixed += jnp.dot(weights.astype(BF16), values, preferred_element_type=F32)
        result = (mixed / sums).astype(BF16)
        for head in range(2):
            out_ref[j * 32:(j + 1) * 32, head * 128:(head + 1) * 128] = result[head * 32:(head + 1) * 32]

    wait(counts_all.at[pl.ds(0, N_CTX - 1)], send_sem.at[0])

    @pl.when(source)
    def _():
        wait(wall, send_sem.at[1])

    @pl.when(jnp.logical_not(source))
    def _():
        wait(wall.at[pl.ds(0, 7)], send_sem.at[1])
        wait(wall.at[0, pl.ds(0, 1)], send_sem.at[1])
        wait(wq, send_sem.at[1])

    wait(inb.at[pl.ds(0, N_CTX - 1)], send_sem.at[2])
    wait(xall.at[pl.ds(0, 7)], send_sem.at[3])
    wait(kvx, send_sem.at[4])
    wait(kvin.at[pl.ds(0, 7)], send_sem.at[5])
    wait(kvall.at[m, co, pl.ds(0, 15)], send_sem.at[6])
    wait(kvall.at[pl.ds(0, 3)], send_sem.at[7])
    wait(kvall.at[m, co], send_sem.at[7])
    wait(pos_all.at[pl.ds(0, N_CTX - 1)], send_sem.at[8])
    wait(qin, send_sem.at[9])


def on_device(hidden, counts, positions, w_query, key_value_weight):
    exponent = np.arange(HEAD_SIZE // 2, dtype=np.float32) * np.float32(2.0 / HEAD_SIZE)
    inverse = np.power(np.float64(rope_base), -exponent.astype(np.float64)).astype(np.float32)
    inverse = jnp.asarray(np.tile(inverse, (8, 2)))
    vmem, hbm = pl.BlockSpec(memory_space=pltpu.VMEM), pl.BlockSpec(memory_space=pltpu.HBM)
    dma = pltpu.SemaphoreType.DMA
    return pl.pallas_call(
        kernel,
        out_shape=jax.ShapeDtypeStruct((ROWS_DEV, 256), BF16),
        in_specs=[vmem, hbm, hbm, hbm, hbm, hbm],
        out_specs=vmem,
        scratch_shapes=[
            pltpu.VMEM((N_CTX, 1, 128), jnp.int32),
            pltpu.VMEM((N_CTX, 3, 128), jnp.int32),
            pltpu.VMEM((8, 128), F32),
            pltpu.VMEM((CAP, 512), BF16),
            pltpu.VMEM((512, 1024), BF16),
            pltpu.VMEM((256, 256), BF16),
            pltpu.VMEM((N_CTX, 48, 128), BF16),
            pltpu.VMEM((N_CTX, 48, 128), BF16),
            pltpu.VMEM((8, ROWS_DEV, 512), BF16),
            pltpu.VMEM((8, 2, 2, 256, 256), BF16),
            pltpu.VMEM((2, 8, 32, 256), F32),
            pltpu.VMEM((2, 8, 32, 256), BF16),
            pltpu.VMEM((8, 32, 256), BF16),
            pltpu.VMEM((8, 32, 256), BF16),
            pltpu.VMEM((8, 32, 256), BF16),
            pltpu.VMEM((4, 2, 16, 32, 256), BF16),
            pltpu.VMEM((2, ROWS_DEV, 128), F32),
            pltpu.VMEM((ROWS_DEV, 256), BF16),
            pltpu.VMEM((ROWS_DEV, 256), BF16),
            pltpu.VMEM((4, 64, 128), BF16),
            dma((5,)),
            dma((10,)),
            dma((1,)),
            dma((1,)),
            dma((1,)),
            dma((34,)),
            dma((2,)),
            dma((1,)),
            dma((16,)),
            dma((3,)),
            dma((17,)),
            dma((1,)),
        ],
        compiler_params=pltpu.CompilerParams(
            collective_id=0, has_side_effects=True, vmem_limit_bytes=63 * 1024 * 1024
        ),
        name="gqa",
    )(
        jnp.broadcast_to(counts[:, None], (1, 128)), inverse, positions.reshape(3, 128),
        hidden, w_query, key_value_weight,
    )


def solution(mesh):
    return jax.shard_map(
        on_device,
        mesh=mesh,
        in_specs=(P("ctx", "tp"), P("ctx"), P("ctx"), P("ctx", "tp"), P("tp", None)),
        out_specs=P("ctx", "tp"),
        check_vma=False,
    )
```

```python
import math

import jax
import jax.numpy as jnp
import numpy as np
from jax import lax
from jax.experimental import pallas as pl
from jax.experimental.pallas import tpu as pltpu
from jax.sharding import PartitionSpec as P

HEAD_SIZE = 128
QUERY_HEADS = 32
KEY_VALUE_HEADS = 4
ROWS_DEV = 128
CAP = 384
N_CTX = 32
N_TP = 16
MESH = pl.DeviceIdType.MESH
rope_base = 500000.0
masked_score = -1e30
BF16 = jnp.bfloat16
F32 = jnp.float32


def iota(shape, dim):
    return lax.broadcasted_iota(jnp.int32, shape, dim)


def kernel(counts_ref, inv_hbm, pos_hbm, hidden_hbm, wq_hbm, kvw_hbm, out_ref,
           counts_all, pos_all, inv_ref, hidden, kvw, wq, outb, inb, xall, wall, kvfull, kvp, kvx, kvs, kvin, kvall,
           trig, qpart, qin, qbuf,
           load_sem, send_sem, info_sem, pos_sem, a2a_sem, w_sem, w_far, w_sib, x_sem, rs_sem, kv_sem, q_sem):
    c = lax.axis_index("ctx")
    t = lax.axis_index("tp")
    xh, z, co = c // 16, lax.rem(c // 2, 8), lax.rem(c, 2)
    y, xl = t // 2, lax.rem(t, 2)
    idx = c // 2
    m = lax.rem(t, 4)

    def ctx_of(h, zz, cc):
        return {"ctx": (h * 8 + zz) * 2 + cc}

    z_near = (ctx_of(xh, lax.rem(z + 1, 8), co), ctx_of(xh, lax.rem(z + 7, 8), co))
    sibling, far_x = ctx_of(xh, z, 1 - co), ctx_of(1 - xh, z, co)
    y_right, y_left = {"tp": lax.rem(y + 1, 8) * 2 + xl}, {"tp": lax.rem(y + 7, 8) * 2 + xl}
    near_x = {"tp": y * 2 + 1 - xl}
    y_pair = {"tp": (y + 1 - 2 * lax.rem(y, 2)) * 2 + xl}

    def send(src, dst, ss, rs, device):
        pltpu.make_async_remote_copy(
            src_ref=src, dst_ref=dst, send_sem=ss, recv_sem=rs, device_id=device, device_id_type=MESH
        ).start()

    def wait(ref, sem):
        pltpu.make_async_copy(ref, ref, sem).wait()

    barrier = pltpu.get_barrier_semaphore()

    @pl.loop(1, N_CTX)
    def _(d):
        pl.semaphore_signal(barrier, inc=1, device_id={"ctx": lax.rem(c + d, N_CTX)}, device_id_type=MESH)

    @pl.loop(1, N_TP)
    def _(d):
        pl.semaphore_signal(barrier, inc=1, device_id={"tp": lax.rem(t + d, N_TP)}, device_id_type=MESH)

    loads = [
        pltpu.make_async_copy(wq_hbm, wq, load_sem.at[0]),
        pltpu.make_async_copy(hidden_hbm, hidden, load_sem.at[1]),
        pltpu.make_async_copy(kvw_hbm, kvw, load_sem.at[2]),
        pltpu.make_async_copy(pos_hbm, pos_all.at[c], load_sem.at[3]),
        pltpu.make_async_copy(inv_hbm, inv_ref, load_sem.at[4]),
    ]
    for load in loads:
        load.start()
    counts_all[c] = counts_ref[...]
    loads[0].wait()
    pl.semaphore_wait(barrier, N_CTX + N_TP - 2)

    @pl.loop(1, N_CTX)
    def _(d):
        send(counts_ref, counts_all.at[c], send_sem.at[0], info_sem.at[0], {"ctx": lax.rem(c + d, N_CTX)})

    source = lax.rem(z + xl, 2) == 0
    other = lax.rem(z + xl, 2)
    relay = other == 1
    halves, sides = (xh, 1 - xh), (xl, 1 - xl)
    one_way = {(0, 0): 0, (0, 1): 1}

    def w_block(r, jj, zz, u):
        return wall.at[halves[r] * 4 + zz // 2, sides[jj], co, pl.ds(u * 128, 128)]

    def w_send(block, device, sem):
        send(block, block, send_sem.at[1], sem, device)

    def ring_sem(r, jj, way, slot, u):
        return w_sem.at[(((r * 2 + jj) * 2 + way) * 2 + slot) * 2 + u]

    def w_start(r, jj, u):
        block = w_block(r, jj, z, u)
        for way in range(2):
            w_send(block, z_near[way], ring_sem(r, jj, way, 0, u))
        w_send(block, far_x, w_far.at[jj])
        w_send(block, sibling, w_sib.at[0])

    def from_z(way, distance):
        return lax.rem(z + 8 - distance, 8) if way == 0 else lax.rem(z + distance, 8)

    def w_slot(r, jj, way, slot, ways):
        for u in range(2):
            block = w_block(r, jj, from_z(way, 2 + 2 * slot - other), u)
            wait(block, ring_sem(r, jj, way, slot, u))
            if way in ways:
                w_send(block, z_near[way], ring_sem(r, jj, way, 1 - other if slot == 0 else 1, u))
            w_send(block, far_x, w_far.at[jj])
            w_send(block, sibling, w_sib.at[0])

    def w_first(r, jj):
        for way in range(2):
            w_slot(r, jj, way, 0, (0, 1))

    def w_first_if(condition, r, jj):
        @pl.when(condition)
        def _():
            w_first(r, jj)

    def w_second_if(condition, r, jj):
        @pl.when(condition)
        def _():
            if condition is source:
                w_slot(r, jj, one_way[r, jj], 1, ())
            else:
                for way in range(2):
                    w_slot(r, jj, way, 1, (one_way[r, jj],))

    def w_second(r, jj):
        @pl.when(source)
        def _():
            w_slot(r, jj, one_way[r, jj], 1, ())

        @pl.when(jnp.logical_not(source))
        def _():
            for way in range(2):
                w_slot(r, jj, way, 1, (one_way[r, jj],))

    @pl.when(source)
    def _():
        wall[xh * 4 + z // 2, xl, co] = wq[...]
        for u in range(2):
            w_start(0, 0, u)
        for u in range(2):
            wait(w_block(0, 1, z, u), w_sem.at[32 + u])
            w_start(0, 1, u)
        w_first(0, 0)

    @pl.when(jnp.logical_not(source))
    def _():
        for u in range(2):
            rows_u = pl.ds(u * 128, 128)
            send(wq.at[rows_u], wall.at[xh * 4 + z // 2, xl, co, rows_u], send_sem.at[1], w_sem.at[32 + u], near_x)
        w_first(0, 0)
        w_first(0, 1)

    wait(counts_all.at[pl.ds(0, N_CTX - 1)], info_sem.at[0])
    counts = counts_all[...].reshape(N_CTX, 128)
    shard = iota((N_CTX, 128), 0)
    own_offset = jnp.sum(jnp.where(shard < c, counts, 0), axis=0, keepdims=True)
    slot = iota((1, CAP), 1)
    place = ((slot + jnp.concatenate([own_offset] * 3, axis=1)) % 32) * 16 + slot // 32
    loads[1].wait()
    for part in range(4):
        chosen = (iota((128, CAP), 0) + 128 * part == place).astype(F32).astype(BF16)
        moved = jnp.dot(chosen, hidden[...], preferred_element_type=F32).reshape(8, 16, 512)
        for k in range(4):
            tall = moved[:, :12, k * 128:(k + 1) * 128]
            outb[pl.ds(part * 8, 8), k * 12:(k + 1) * 12, :] = tall.astype(BF16)
    inb[c] = outb[c]

    @pl.loop(1, N_CTX)
    def _(d):
        peer = lax.rem(c + d, N_CTX)
        send(outb.at[peer], inb.at[c], send_sem.at[2], a2a_sem.at[0], {"ctx": peer})

    loads[3].wait()

    @pl.loop(1, N_CTX)
    def _(d):
        send(pos_all.at[c], pos_all.at[c], send_sem.at[8], pos_sem.at[0], {"ctx": lax.rem(c + d, N_CTX)})

    column = iota((1, 1536), 1)
    column_shard = (column * 1366) >> 16
    in_shard = column - column_shard * 48
    column_part = (in_shard * 5462) >> 16
    column_turn = in_shard - column_part * 12
    counts_wide = jnp.concatenate([counts] * 12, axis=1)
    shard_wide = iota((N_CTX, 1536), 0)
    first = jnp.sum(jnp.where(shard_wide < column_shard, counts_wide, 0), axis=0, keepdims=True)
    number = jnp.sum(jnp.where(shard_wide == column_shard, counts_wide, 0), axis=0, keepdims=True)
    low_rank = first + 32 * column_turn
    high_rank = jnp.minimum(low_rank + 32, first + number)
    pick_rank = iota((ROWS_DEV, 1536), 0) * N_CTX + c
    pick = (pick_rank >= low_rank) & (pick_rank < high_rank)
    wait(inb.at[pl.ds(0, N_CTX - 1)], a2a_sem.at[0])
    arrived = inb[...].reshape(1536, 128)
    for k in range(4):
        chosen = (pick & (column_part == k)).astype(F32).astype(BF16)
        xall[y, :, k * 128:(k + 1) * 128] = jnp.dot(chosen, arrived, preferred_element_type=F32).astype(BF16)

    def x_send(ref, device, sem):
        send(ref, ref, send_sem.at[3], sem, device)

    def x_part(yy, u):
        return xall.at[yy, pl.ds(u * 64, 64)]

    for u in range(2):
        x_send(x_part(y, u), y_right, x_sem.at[u])
        x_send(x_part(y, u), y_left, x_sem.at[8 + u])

    def x_step(s):
        for u in range(2):
            for way, device in ((0, y_right), (1, y_left)):
                if s == 3 and u != way:
                    continue
                part = x_part(lax.rem(y + (7 - s if way == 0 else 1 + s), 8), u)
                wait(part, x_sem.at[way * 8 + s * 2 + u])
                if s < 2 or (s == 2 and u == way):
                    x_send(part, device, x_sem.at[way * 8 + (s + 1) * 2 + u])

    loads[2].wait()
    rows = xall[y]
    for g in range(KEY_VALUE_HEADS):
        partial = jnp.dot(rows, kvw[:, g * 256:(g + 1) * 256], preferred_element_type=F32)
        for quarter in range(4):
            piece = partial[quarter * 32:(quarter + 1) * 32]
            kvfull[quarter % 2, g * 2 + quarter // 2] = piece
            kvp[quarter % 2, g * 2 + quarter // 2] = piece.astype(BF16)
    for h in range(2):
        part = pl.ds(h * 4, 4)
        send(kvp.at[1 - xl, part], kvx.at[part], send_sem.at[4], rs_sem.at[h], near_x)

    def rotate(u, cosine, sine):
        return u * cosine + pltpu.roll(u, HEAD_SIZE // 2, 1) * sine

    own_kv = kvall.at[m, co, idx]
    z_half = z // 4

    def kv_where(n):
        return halves[n // 2], z_half if n % 2 == 0 else 1 - z_half

    def kv_send(ref, device, sem):
        send(ref, ref, send_sem.at[7], sem, device)

    mx, my, mxy = m + 1 - 2 * xl, lax.rem(m + 2, 4), 3 - m

    def kv_chunk(b, n):
        hh, half_z = kv_where(n)
        return kvall.at[b, co, pl.ds(pl.multiple_of(hh * 8 + half_z * 4, 4), 4)]

    def kv_out(n):
        wait(kvall.at[m, co, pl.ds(0, 4 if n else 3)], kv_sem.at[n])
        block = kv_chunk(m, n)
        kv_send(block, y_pair, kv_sem.at[4 + n])
        kv_send(block, near_x, kv_sem.at[8 + n])
        kv_send(block, sibling, kv_sem.at[16])

    def kv_mid(n):
        block = kv_chunk(mx if n % 2 else my, n)
        wait(block, kv_sem.at[8 + n if n % 2 else 4 + n])
        kv_send(block, y_pair if n % 2 else near_x, kv_sem.at[12 + n])
        kv_send(block, sibling, kv_sem.at[16])

    def kv_last(n):
        for block, k in ((kv_chunk(my if n % 2 else mx, n), 4 + n if n % 2 else 8 + n), (kv_chunk(mxy, n), 12 + n)):
            wait(block, kv_sem.at[k])
            kv_send(block, sibling, kv_sem.at[16])

    def partial_queries(j):
        def add_block(k, acc):
            return acc + jnp.dot(xall[k], wall[k, j].reshape(512, 256), preferred_element_type=F32)

        return lax.fori_loop(0, 8, add_block, jnp.zeros((ROWS_DEV, 256), F32), unroll=True)

    w_first_if(source, 0, 1)
    w_second(0, 0)
    wait(kvx.at[pl.ds(0, 4)], rs_sem.at[0])
    kvs[0:4] = (kvfull[xl, 0:4] + kvx[0:4].astype(F32)).astype(BF16)

    def kvs_send(peer):
        @pl.when(peer == y)
        def _():
            kvin[y] = kvs[y]

        @pl.when(peer != y)
        def _():
            send(kvs.at[peer], kvin.at[y], send_sem.at[5], rs_sem.at[2], {"tp": peer * 2 + xl})

    @pl.loop(0, 4)
    def _(d):
        kvs_send(lax.rem(y + d, 4))

    wait(kvx.at[pl.ds(4, 4)], rs_sem.at[1])
    kvs[4:8] = (kvfull[xl, 4:8] + kvx[4:8].astype(F32)).astype(BF16)

    @pl.loop(0, 4)
    def _(d):
        kvs_send(4 + lax.rem(y + d, 4))

    x_step(0)
    w_second(0, 1)
    x_step(1)
    loads[4].wait()
    wait(pos_all.at[pl.ds(0, N_CTX - 1)], pos_sem.at[0])
    lane = iota((N_CTX, 128), 1)
    first_of = jnp.sum(jnp.where(shard < lane, counts, 0), axis=0, keepdims=True)
    number_of = jnp.sum(jnp.where(shard == lane, counts, 0), axis=0, keepdims=True)
    rank = iota((ROWS_DEV, 128), 0) * N_CTX + c
    from_shard = (rank >= first_of) & (rank < first_of + number_of)
    within = jnp.sum(jnp.where(from_shard, rank - first_of, 0).astype(F32), axis=1, keepdims=True)
    holder = from_shard.astype(F32).astype(BF16)[:, :N_CTX]
    picked = jnp.zeros((ROWS_DEV, 128), F32)
    for part in range(3):
        place_of = pos_all[:, part, :]
        high = jnp.dot(holder, (place_of // 256).astype(F32).astype(BF16), preferred_element_type=F32)
        low = jnp.dot(holder, (place_of % 256).astype(F32).astype(BF16), preferred_element_type=F32)
        here = iota((ROWS_DEV, 128), 1).astype(F32) + 128.0 * part == within
        picked += jnp.where(here, high * 256.0 + low, 0.0)
    angles = jnp.sum(picked, axis=1, keepdims=True) * inv_ref[0:1, :]
    trig[0] = jnp.cos(angles)
    trig[1] = jnp.where(iota((ROWS_DEV, 128), 1) < HEAD_SIZE // 2, -1.0, 1.0) * jnp.sin(angles)

    mine_kv = pl.ds(pl.multiple_of(m * 32, 32), 32)
    wait(kvin.at[pl.ds(0, 7)], rs_sem.at[2])
    total = jnp.zeros((32, 256), F32)
    for s in range(8):
        total += kvin[s].astype(F32)
    kvall[m, co, idx, :, :HEAD_SIZE] = rotate(total[:, :HEAD_SIZE], trig[0, mine_kv], trig[1, mine_kv]).astype(BF16)
    kvall[m, co, idx, :, HEAD_SIZE:] = total[:, HEAD_SIZE:].astype(BF16)

    for n in range(4):
        hh, half_z = kv_where(n)

        @pl.loop(1 if n == 0 else 0, 4)
        def _(d):
            send(own_kv, own_kv, send_sem.at[6], kv_sem.at[n], ctx_of(hh, half_z * 4 + lax.rem(z + d, 4), co))

    x_step(2)
    kv_out(0)
    kv_out(1)
    kv_mid(0)
    wait(wall.at[pl.ds(0, 1)], w_far.at[0])
    w_send(wall.at[pl.ds((1 - xh) * 4, 4), sides[0], co], sibling, w_sib.at[0])
    wait(wall.at[pl.ds(0, 1)], w_far.at[1])
    w_send(wall.at[pl.ds((1 - xh) * 4, 4), sides[1], co], sibling, w_sib.at[0])
    kv_out(2)
    kv_mid(1)
    kv_out(3)
    x_step(3)
    kv_mid(2)
    wait(wall.at[pl.ds(0, 4)], w_sib.at[0])
    qpart[...] = partial_queries(1 - xl).astype(BF16)
    send(qpart, qin, send_sem.at[9], q_sem.at[0], near_x)
    kv_last(0)
    kv_mid(3)
    kv_last(1)
    q = partial_queries(xl)
    kv_last(2)
    kv_last(3)
    wait(qin, q_sem.at[0])
    q = q + qin[...].astype(F32)
    for head in range(2):
        turned = rotate(q[:, head * 128:(head + 1) * 128], trig[0], trig[1]).astype(BF16)
        for j in range(4):
            qbuf[j, head * 32:(head + 1) * 32, :] = turned[j * 32:(j + 1) * 32]

    wait(kvall.at[pl.ds(0, 2)], kv_sem.at[16])

    scale = 1.0 / math.sqrt(HEAD_SIZE)
    key_index = iota((64, 1024), 1)
    query_row = iota((64, 1024), 0) % 32
    key_row = key_index % 32
    key_ctx = (key_index // 32 % 16) * 2 + key_index // 512
    seen = (key_row < query_row) | ((key_row == query_row) & (key_ctx <= c))
    for j in range(4):
        scores = []
        for b in range(j + 1):
            keys = kvall[b, :, :, :, :HEAD_SIZE].reshape(1024, HEAD_SIZE)
            part = lax.dot_general(qbuf[j], keys, (((1,), (1,)), ((), ())), preferred_element_type=F32) * scale
            scores.append(jnp.where(seen, part, masked_score) if b == j else part)
        largest = jnp.max(scores[0], axis=1, keepdims=True)
        for part in scores[1:]:
            largest = jnp.maximum(largest, jnp.max(part, axis=1, keepdims=True))
        sums = jnp.zeros((64, 1), F32)
        mixed = jnp.zeros((64, HEAD_SIZE), F32)
        for b in range(j + 1):
            weights = jnp.exp(scores[b] - largest)
            if b == j:
                weights = jnp.where(seen, weights, 0.0)
            sums += jnp.sum(weights, axis=1, keepdims=True)
            values = kvall[b, :, :, :, HEAD_SIZE:].reshape(1024, HEAD_SIZE)
            mixed += jnp.dot(weights.astype(BF16), values, preferred_element_type=F32)
        result = (mixed / sums).astype(BF16)
        for head in range(2):
            out_ref[j * 32:(j + 1) * 32, head * 128:(head + 1) * 128] = result[head * 32:(head + 1) * 32]

    wait(counts_all.at[pl.ds(0, N_CTX - 1)], send_sem.at[0])

    @pl.when(source)
    def _():
        wait(wall, send_sem.at[1])

    @pl.when(jnp.logical_not(source))
    def _():
        wait(wall.at[pl.ds(0, 7)], send_sem.at[1])
        wait(wall.at[0, pl.ds(0, 1)], send_sem.at[1])
        wait(wq, send_sem.at[1])

    wait(inb.at[pl.ds(0, N_CTX - 1)], send_sem.at[2])
    wait(xall.at[pl.ds(0, 7)], send_sem.at[3])
    wait(kvx, send_sem.at[4])
    wait(kvin.at[pl.ds(0, 7)], send_sem.at[5])
    wait(kvall.at[m, co, pl.ds(0, 15)], send_sem.at[6])
    wait(kvall.at[pl.ds(0, 3)], send_sem.at[7])
    wait(kvall.at[m, co], send_sem.at[7])
    wait(pos_all.at[pl.ds(0, N_CTX - 1)], send_sem.at[8])
    wait(qin, send_sem.at[9])


def on_device(hidden, counts, positions, w_query, key_value_weight):
    exponent = np.arange(HEAD_SIZE // 2, dtype=np.float32) * np.float32(2.0 / HEAD_SIZE)
    inverse = np.power(np.float64(rope_base), -exponent.astype(np.float64)).astype(np.float32)
    inverse = jnp.asarray(np.tile(inverse, (8, 2)))
    vmem, hbm = pl.BlockSpec(memory_space=pltpu.VMEM), pl.BlockSpec(memory_space=pltpu.HBM)
    dma = pltpu.SemaphoreType.DMA
    return pl.pallas_call(
        kernel,
        out_shape=jax.ShapeDtypeStruct((ROWS_DEV, 256), BF16),
        in_specs=[vmem, hbm, hbm, hbm, hbm, hbm],
        out_specs=vmem,
        scratch_shapes=[
            pltpu.VMEM((N_CTX, 1, 128), jnp.int32),
            pltpu.VMEM((N_CTX, 3, 128), jnp.int32),
            pltpu.VMEM((8, 128), F32),
            pltpu.VMEM((CAP, 512), BF16),
            pltpu.VMEM((512, 1024), BF16),
            pltpu.VMEM((256, 256), BF16),
            pltpu.VMEM((N_CTX, 48, 128), BF16),
            pltpu.VMEM((N_CTX, 48, 128), BF16),
            pltpu.VMEM((8, ROWS_DEV, 512), BF16),
            pltpu.VMEM((8, 2, 2, 256, 256), BF16),
            pltpu.VMEM((2, 8, 32, 256), F32),
            pltpu.VMEM((2, 8, 32, 256), BF16),
            pltpu.VMEM((8, 32, 256), BF16),
            pltpu.VMEM((8, 32, 256), BF16),
            pltpu.VMEM((8, 32, 256), BF16),
            pltpu.VMEM((4, 2, 16, 32, 256), BF16),
            pltpu.VMEM((2, ROWS_DEV, 128), F32),
            pltpu.VMEM((ROWS_DEV, 256), BF16),
            pltpu.VMEM((ROWS_DEV, 256), BF16),
            pltpu.VMEM((4, 64, 128), BF16),
            dma((5,)),
            dma((10,)),
            dma((1,)),
            dma((1,)),
            dma((1,)),
            dma((34,)),
            dma((2,)),
            dma((1,)),
            dma((16,)),
            dma((3,)),
            dma((17,)),
            dma((1,)),
        ],
        compiler_params=pltpu.CompilerParams(
            collective_id=0, has_side_effects=True, vmem_limit_bytes=63 * 1024 * 1024
        ),
        name="gqa",
    )(
        jnp.broadcast_to(counts[:, None], (1, 128)), inverse, positions.reshape(3, 128),
        hidden, w_query, key_value_weight,
    )


def solution(mesh):
    return jax.shard_map(
        on_device,
        mesh=mesh,
        in_specs=(P("ctx", "tp"), P("ctx"), P("ctx"), P("ctx", "tp"), P("tp", None)),
        out_specs=P("ctx", "tp"),
        check_vma=False,
    )
```
